128 devices in a mesh: gx: 8 (over x, core), gy: 16 (over z, y).
Axes of the slice: x: 4, y: 4, z: 4, core: 2. Of those that a mesh axis runs over, the one named last changes fastest.
Arguments:
- sources: float32 [16, 4194304], P(None, ('gx', 'gy')), may hold values from -6 to 6
- leaf_basis: float32 [4096, 48, 1024], P(('gx', 'gy')), may hold values from -0.1875 to 0.1875
- level_blocks: float32 [8, 2, 48, 48, 4096], P(None, None, None, None, ('gx', 'gy')), may hold values from -0.625 to 0.625
- out_basis: float32 [4096, 48, 1024], P(('gx', 'gy')), may hold values from -0.875 to 0.875
Outputs:
- applied: float32 [16, 4194304], P(None, ('gx', 'gy'))
The draws below stay inside these ranges and needn't reach their ends.
All inputs are finite; a program needn't handle non-finite values.
Results may differ from the reference program's by a relative error of at most 0.00011.
Values sent between devices are 32-bit elements; how exact they have to be, the bound alone decides.
A program may use at most 128 MiB of HBM per device.

```python
import jax
import jax.numpy as jnp
from jax import lax

RANK = 48
SOURCES = 16
LEAF_PTS = 1024
BOXES_DEV = 32
LOCAL = 1
LEVELS = 8
BOXES = 4096
POINTS = 4194304
N_GX = 8
N_GY = 16


def steps_of(key, dims, cuts, smallest, high):
    loudness = 1.0
    for position, blocks in cuts:
        steps = jax.random.uniform(jax.random.fold_in(jax.random.fold_in(key, 6), position), (blocks,), jnp.float32, smallest / len(cuts), high / len(cuts))
        loudness = loudness * jnp.repeat(jnp.exp(steps), dims[position] // blocks).reshape((-1,) + (1,) * (len(dims) - 1 - position))
    return loudness


def normal_values(stream_key, dims, width, bound, pieces=(), held_as=jnp.bfloat16):
    gain = steps_of(stream_key, dims, pieces, -0.22, 0.18) if pieces else 1.0
    array = jax.random.normal(stream_key, dims, jnp.float32) * width * gain
    return jnp.minimum(jnp.maximum(array, -bound), bound).astype(held_as)


def setup_inputs(seed: int = 0) -> dict:
    splits = jax.random.split(jax.random.key(seed), 5)
    sources = normal_values(splits[0], (SOURCES, POINTS), 1.0, 6.0, ((1, 128),), jnp.float32)
    leaf_basis = normal_values(splits[1], (BOXES, RANK, LEAF_PTS), LEAF_PTS ** -0.5, 0.1875, ((0, 128),), jnp.float32)
    level_blocks = normal_values(splits[2], (LEVELS, 2, RANK, RANK, BOXES), (2 * RANK) ** -0.5, 0.625, ((4, 128),), jnp.float32)
    out_basis = normal_values(splits[3], (BOXES, RANK, LEAF_PTS), RANK ** -0.5, 0.875, ((0, 128),), jnp.float32)
    return dict(sources=sources, leaf_basis=leaf_basis, level_blocks=level_blocks, out_basis=out_basis)


def partner_of(state, stride):
    rank_n, count, total = state.shape
    view = state.reshape(rank_n, count, total // (2 * stride), 2, stride)
    return jnp.flip(view, 3).reshape(rank_n, count, total)


def reference(sources, leaf_basis, level_blocks, out_basis):
    points = sources.reshape(SOURCES, BOXES, LEAF_PTS)
    state = jnp.einsum("sgp,grp->rsg", points, leaf_basis, precision=lax.Precision.HIGHEST)
    xbits = int(N_GX).bit_length() - 1
    ybits = int(N_GY).bit_length() - 1
    strides = [2 ** level for level in range(LOCAL)]
    strides = strides + [BOXES_DEV * 2 ** j for j in range(ybits)]
    strides = strides + [BOXES_DEV * N_GY * 2 ** j for j in range(xbits)]
    for level, stride in enumerate(strides):
        other = partner_of(state, stride)
        state = jnp.einsum("abg,bsg->asg", level_blocks[level, 0], state, precision=lax.Precision.HIGHEST) + jnp.einsum("abg,bsg->asg", level_blocks[level, 1], other, precision=lax.Precision.HIGHEST)
    share = BOXES_DEV // N_GY
    regrouped = state.reshape(RANK, SOURCES, N_GX, N_GY, N_GY, share).transpose(0, 1, 2, 4, 3, 5).reshape(RANK, SOURCES, BOXES)
    applied = jnp.einsum("grp,rsg->sgp", out_basis, regrouped, precision=lax.Precision.HIGHEST)
    return applied.reshape(SOURCES, POINTS)
```

```python
import functools

import jax
import jax.numpy as jnp
from jax import lax
from jax.experimental import pallas as pl
from jax.experimental.pallas import tpu as pltpu
from jax.sharding import PartitionSpec as P

F32 = jnp.float32
BF16 = jnp.bfloat16
LANES = 128
CHUNK = 4


def flipped(index, bit):
    return index + bit * (1 - 2 * (lax.div(index, bit) % 2))


def crossed(index, mask):
    bit = 1
    while bit <= mask:
        if mask & bit:
            index = flipped(index, bit)
        bit *= 2
    return index


def split(value):
    high = value.astype(BF16)
    return high, (value - high.astype(F32)).astype(BF16)


def stacked(value):
    high, low = split(value)
    return jnp.concatenate(
        [
            jnp.concatenate([high, high], 1),
            jnp.concatenate([low, jnp.zeros_like(low)], 1),
        ],
        0,
    )


def across(left, right):
    return lax.dot_general(left, right, (((1,), (1,)), ((), ())), preferred_element_type=F32)


def kernel(
    n_gx, n_gy, rank,
    src, leaf, blocks, basis, out,
    src_v, leaf_v, raw, tiles, state, far, moved, wide,
    src_sem, leaf_sem, raw_sem, basis_sem, send_sem, recv_sem, out_sem, in_sem,
):
    pairs = leaf.shape[0]
    count = src.shape[0]
    points = leaf.shape[2]
    levels = blocks.shape[0] // 2
    chunks = pairs // CHUNK
    both = 2 * rank
    gx, gy = lax.axis_index("gx"), lax.axis_index("gy")
    lane = lax.broadcasted_iota(jnp.int32, (count, both), 1)
    first_box = lane < rank

    def partner(level):
        bit = 2 ** (level - 1)
        if bit < n_gy:
            return gx, flipped(gy, bit)
        return flipped(gx, bit // n_gy), gy

    def src_copy(j):
        width = CHUNK * 2 * points
        return pltpu.make_async_copy(
            src.at[:, pl.ds(pl.multiple_of(j * width, width), width)], src_v.at[j], src_sem.at[j]
        )

    def leaf_copy(j):
        part = pl.ds(j * CHUNK, CHUNK)
        return pltpu.make_async_copy(leaf.at[part], leaf_v.at[part], leaf_sem.at[j])

    def basis_copy(j):
        part = pl.ds(j * CHUNK, CHUNK)
        return pltpu.make_async_copy(basis.at[part], leaf_v.at[part], basis_sem.at[j])

    def raw_copy(i):
        return pltpu.make_async_copy(blocks.at[i], raw.at[i], raw_sem.at[i])

    def exchange(level, j):
        part = pl.ds(j * CHUNK, CHUNK)
        return pltpu.make_async_remote_copy(
            src_ref=state.at[level, part],
            dst_ref=far.at[level, part],
            send_sem=send_sem.at[level, j],
            recv_sem=recv_sem.at[level, j],
            device_id=partner(level),
            device_id_type=pl.DeviceIdType.MESH,
        )

    def handover(b):
        return pltpu.make_async_remote_copy(
            src_ref=state.at[levels, b],
            dst_ref=moved.at[gy],
            send_sem=out_sem.at[b],
            recv_sem=in_sem.at[gy],
            device_id=(gx, b),
            device_id_type=pl.DeviceIdType.MESH,
        )

    def arrival(a):
        return pltpu.make_async_remote_copy(
            src_ref=state.at[levels, a],
            dst_ref=moved.at[a],
            send_sem=out_sem.at[a],
            recv_sem=in_sem.at[a],
            device_id=(gx, a),
            device_id_type=pl.DeviceIdType.MESH,
        )

    barrier = pltpu.get_barrier_semaphore()
    for level in range(1, levels):
        pl.semaphore_signal(barrier, inc=1, device_id=partner(level), device_id_type=pl.DeviceIdType.MESH)

    raw_copy(0).start()
    raw_copy(1).start()
    ahead = 2
    for j in range(min(ahead, chunks)):
        src_copy(j).start()
        leaf_copy(j).start()

    def blank(i, carry):
        state[i] = jnp.zeros_like(state[i])
        return carry

    lax.fori_loop(0, levels + 1, blank, 0)

    def lay(level, which, p):
        gap = jnp.zeros((rank, LANES - both), F32)
        empty = jnp.zeros((rank, rank), F32)
        total = 2 * pairs
        for c in range(2):
            own = raw[2 * level + which, pl.ds(2 * p + c, rank, stride=total), :]
            if level == 0:
                other = raw[1, pl.ds(2 * p + c, rank, stride=total), :]
            else:
                other = empty
            full = jnp.concatenate([own, other, gap] if c == 0 else [other, own, gap], 1)
            high, low = split(full)
            tiles[level, which, p, c * rank : (c + 1) * rank, :LANES] = high
            tiles[level, which, p, c * rank : (c + 1) * rank, LANES:] = low

    def lay_level(level):
        def step(i, carry):
            for q in range(2):
                for which in range(1 if level == 0 else 2):
                    lay(level, which, 2 * i + q)
            return carry

        raw_copy(2 * level).wait()
        raw_copy(2 * level + 1).wait()
        lax.fori_loop(0, pairs // 2, step, 0)

    lay_level(0)

    def compress(j, carry):
        src_copy(j).wait()
        leaf_copy(j).wait()

        @pl.when(j + ahead < chunks)
        def _():
            src_copy(j + ahead).start()
            leaf_copy(j + ahead).start()

        for q in range(CHUNK):
            p = j * CHUNK + q
            high, low = split(leaf_v[p])
            h0, l0 = split(src_v[j, :, 2 * q * points : (2 * q + 1) * points])
            h1, l1 = split(src_v[j, :, (2 * q + 1) * points : (2 * q + 2) * points])
            main = across(jnp.concatenate([h0, h1, l0, l1], 0), high)
            rest = across(jnp.concatenate([h0, h1], 0), low)
            total = main[: 2 * count] + main[2 * count :] + rest
            state[0, p, :, :both] = jnp.where(first_box, total[:count], total[count:])
        for q in range(CHUNK):
            p = j * CHUNK + q
            product = across(stacked(state[0, p]), tiles[0, 0, p])
            state[1, p, :, :both] = product[:count] + product[count:]

        @pl.when(j == 0)
        def _():
            pl.semaphore_wait(barrier, levels - 1)

        exchange(1, j).start()
        return carry

    lax.fori_loop(0, chunks, compress, 0)
    for i in range(2, 2 * levels):
        raw_copy(i).start()
    for j in range(chunks):
        basis_copy(j).start()
    lay_level(1)

    for level in range(1, levels):

        def combine(j, carry, level=level):
            exchange(level, j).wait_recv()
            for q in range(CHUNK):
                p = j * CHUNK + q
                product = across(stacked(state[level, p]), tiles[level, 0, p])
                product += across(stacked(far[level, p]), tiles[level, 1, p])
                state[level + 1, p, :, :both] = product[:count] + product[count:]
            if level + 1 < levels:
                exchange(level + 1, j).start()
            else:
                for q in range(CHUNK):
                    b = j * CHUNK + q

                    @pl.when(b != gy)
                    def _():
                        handover(b).start()

            return carry

        lax.fori_loop(0, chunks, combine, 0)
        if level + 1 < levels:
            lay_level(level + 1)
        if level == 1:

            def spread(j, carry):
                basis_copy(j).wait()
                for q in range(CHUNK):
                    p = j * CHUNK + q
                    high, low = split(leaf_v[p])
                    wide[p, :both] = high
                    wide[p, both:] = low
                return carry

            lax.fori_loop(0, chunks, spread, 0)

    moved[gy] = state[levels, gy]
    hops = [0, 1, 2, 1]
    order = sorted(range(n_gy), key=lambda d: hops[d % 4] + hops[d // 4 % 4])
    for d in order:
        a = crossed(gy, d)
        if d:
            arrival(a).wait_recv()
        high, low = split(moved[a][:, :both])
        none = jnp.zeros_like(high)
        rows = []
        for mine in (first_box, jnp.logical_not(first_box)):
            kept = jnp.where(mine, high, none)
            rows.append(jnp.concatenate([kept, kept], 1))
            rows.append(jnp.concatenate([jnp.where(mine, low, none), none], 1))
        product = jnp.dot(jnp.concatenate(rows, 0), wide[a], preferred_element_type=F32)
        for c in range(2):
            at = pl.multiple_of((2 * a + c) * points, points)
            out[:, pl.ds(at, points)] = (
                product[2 * c * count : (2 * c + 1) * count]
                + product[(2 * c + 1) * count : (2 * c + 2) * count]
            )

    def drain(j, carry):
        for level in range(1, levels):
            exchange(level, j).wait_send()
        return carry

    lax.fori_loop(0, chunks, drain, 0)

    def drain_out(b, carry):
        @pl.when(b != gy)
        def _():
            handover(b).wait_send()

        return carry

    lax.fori_loop(0, n_gy, drain_out, 0)


def body(n_gx, n_gy, sources, leaf_basis, level_blocks, out_basis):
    boxes, rank, points = leaf_basis.shape
    count = sources.shape[0]
    levels = level_blocks.shape[0]
    pairs = boxes // 2
    chunks = pairs // CHUNK
    leaf = leaf_basis.reshape(pairs, 2 * rank, points)
    basis = out_basis.reshape(pairs, 2 * rank, points)
    blocks = level_blocks.transpose(0, 1, 2, 4, 3).reshape(2 * levels, rank * boxes, rank)
    dma = pltpu.SemaphoreType.DMA
    anywhere = pl.BlockSpec(memory_space=pl.ANY)
    return pl.pallas_call(
        functools.partial(kernel, n_gx, n_gy, rank),
        out_shape=jax.ShapeDtypeStruct((count, boxes * points), F32),
        in_specs=[anywhere] * 4,
        out_specs=pl.BlockSpec(memory_space=pltpu.VMEM),
        scratch_shapes=[
            pltpu.VMEM((chunks, count, CHUNK * 2 * points), F32),
            pltpu.VMEM((pairs, 2 * rank, points), F32),
            pltpu.VMEM((2 * levels, rank * boxes, rank), F32),
            pltpu.VMEM((levels, 2, pairs, 2 * rank, 2 * LANES), BF16),
            pltpu.VMEM((levels + 1, pairs, count, LANES), F32),
            pltpu.VMEM((levels, pairs, count, LANES), F32),
            pltpu.VMEM((n_gy, count, LANES), F32),
            pltpu.VMEM((pairs, 4 * rank, points), BF16),
            dma((chunks,)),
            dma((chunks,)),
            dma((2 * levels,)),
            dma((chunks,)),
            dma((levels, chunks)),
            dma((levels, chunks)),
            dma((n_gy,)),
            dma((n_gy,)),
        ],
        compiler_params=pltpu.CompilerParams(
            collective_id=0, has_side_effects=True, vmem_limit_bytes=60 * 2**20
        ),
        name="sweep",
    )(sources, leaf, blocks, basis)


def solution(mesh):
    placed = (
        P(None, ("gx", "gy")),
        P(("gx", "gy"), None, None),
        P(None, None, None, None, ("gx", "gy")),
        P(("gx", "gy"), None, None),
    )
    return jax.shard_map(
        functools.partial(body, mesh.shape["gx"], mesh.shape["gy"]),
        mesh=mesh, in_specs=placed, out_specs=P(None, ("gx", "gy")), check_vma=False,
    )
```

```python
import functools

import jax
import jax.numpy as jnp
from jax import lax
from jax.experimental import pallas as pl
from jax.experimental.pallas import tpu as pltpu
from jax.sharding import PartitionSpec as P

F32 = jnp.float32
BF16 = jnp.bfloat16
LANES = 128
SHARES = (4, 4, 4, 4)


def parts_of(pairs):
    if sum(SHARES) != pairs:
        return [(p, 1) for p in range(pairs)]
    return [(sum(SHARES[:j]), n) for j, n in enumerate(SHARES)]


def flipped(index, bit):
    return index + bit * (1 - 2 * (lax.div(index, bit) % 2))


def crossed(index, mask):
    bit = 1
    while bit <= mask:
        if mask & bit:
            index = flipped(index, bit)
        bit *= 2
    return index


def split(value):
    high = value.astype(BF16)
    return high, (value - high.astype(F32)).astype(BF16)


def stacked(value):
    high, low = split(value)
    return jnp.concatenate(
        [
            jnp.concatenate([high, high], 1),
            jnp.concatenate([low, jnp.zeros_like(low)], 1),
        ],
        0,
    )


def across(left, right):
    return lax.dot_general(left, right, (((1,), (1,)), ((), ())), preferred_element_type=F32)


def kernel(
    n_gx, n_gy, rank,
    src, leaf, blocks, basis, out,
    src_v, leaf_v, raw, tiles, state, far, held, moved, wide,
    src_sem, leaf_sem, raw_sem, basis_sem, send_sem, recv_sem, out_sem, in_sem,
):
    pairs = leaf.shape[0]
    count = src.shape[0]
    points = leaf.shape[2]
    levels = blocks.shape[0] // 2
    parts = parts_of(pairs)
    both = 2 * rank
    pitch = raw.shape[2]
    gx, gy = lax.axis_index("gx"), lax.axis_index("gy")
    lane = lax.broadcasted_iota(jnp.int32, (count, both), 1)
    first_box = lane < rank

    def partner(level):
        bit = 2 ** (level - 1)
        if bit < n_gy:
            return gx, flipped(gy, bit)
        return flipped(gx, bit // n_gy), gy

    def src_copy(j):
        first, n = parts[j]
        here = pl.ds(first * 2 * points, n * 2 * points)
        return pltpu.make_async_copy(src.at[:, here], src_v.at[:, here], src_sem.at[j])

    def leaf_copy(j):
        here = pl.ds(*parts[j])
        return pltpu.make_async_copy(leaf.at[here], leaf_v.at[here], leaf_sem.at[j])

    def basis_copy(j):
        here = pl.ds(*parts[j])
        return pltpu.make_async_copy(basis.at[here], leaf_v.at[here], basis_sem.at[j])

    def raw_copy(i):
        return pltpu.make_async_copy(
            blocks.at[i], raw.at[i, :, pl.ds(0, 2 * pairs), :], raw_sem.at[i]
        )

    def exchange(level, j):
        here = pl.ds(*parts[j])
        return pltpu.make_async_remote_copy(
            src_ref=state.at[level, here],
            dst_ref=far.at[level, here],
            send_sem=send_sem.at[level, j],
            recv_sem=recv_sem.at[level, j],
            device_id=partner(level),
            device_id_type=pl.DeviceIdType.MESH,
        )

    def handover(b):
        return pltpu.make_async_remote_copy(
            src_ref=state.at[levels, b],
            dst_ref=moved.at[gy],
            send_sem=out_sem.at[b],
            recv_sem=in_sem.at[gy],
            device_id=(gx, b),
            device_id_type=pl.DeviceIdType.MESH,
        )

    def arrival(a):
        return pltpu.make_async_remote_copy(
            src_ref=state.at[levels, a],
            dst_ref=moved.at[a],
            send_sem=out_sem.at[a],
            recv_sem=in_sem.at[a],
            device_id=(gx, a),
            device_id_type=pl.DeviceIdType.MESH,
        )

    barrier = pltpu.get_barrier_semaphore()
    for level in range(1, levels):
        pl.semaphore_signal(barrier, inc=1, device_id=partner(level), device_id_type=pl.DeviceIdType.MESH)

    def load(j):
        src_copy(j).start()
        leaf_copy(j).start()

    load(0)
    raw_copy(0).start()
    raw_copy(1).start()
    load(1)

    def blank(i, carry):
        state[i] = jnp.zeros_like(state[i])
        return carry

    lax.fori_loop(0, levels + 1, blank, 0)

    def lay(level, which, p):
        gap = jnp.zeros((rank, LANES - rank), F32)

        def rows_of(i, c):
            rows = raw.at[i].reshape(rank * pitch, rank)
            own = rows[pl.ds(2 * p + c, rank, stride=pitch), :]
            return jnp.concatenate([own, gap], 1)

        for c in range(2):
            full = rows_of(2 * level + which, c)
            if c:
                full = pltpu.roll(full, rank, 1)
            if level == 0:
                other = rows_of(1, c)
                full += other if c else pltpu.roll(other, rank, 1)
            high, low = split(full)
            tiles[level, which, p, c * rank : (c + 1) * rank, :LANES] = high
            tiles[level, which, p, c * rank : (c + 1) * rank, LANES:] = low

    def lay_level(level):
        def step(i, carry):
            for q in range(2):
                for which in range(1 if level == 0 else 2):
                    lay(level, which, 2 * i + q)
            return carry

        raw_copy(2 * level).wait()
        raw_copy(2 * level + 1).wait()
        lax.fori_loop(0, pairs // 2, step, 0)

    def compress(p):
        high, low = split(leaf_v[p])
        h0, l0 = split(src_v[:, 2 * p * points : (2 * p + 1) * points])
        h1, l1 = split(src_v[:, (2 * p + 1) * points : (2 * p + 2) * points])
        main = across(jnp.concatenate([h0, h1, l0, l1], 0), high)
        rest = across(jnp.concatenate([h0, h1], 0), low)
        total = main[: 2 * count] + main[2 * count :] + rest
        state[0, p, :, :both] = jnp.where(first_box, total[:count], total[count:])

    def pair_up(p):
        product = across(stacked(state[0, p]), tiles[0, 0, p])
        state[1, p, :, :both] = product[:count] + product[count:]

    def own_term(level):
        def step(i, carry):
            for q in range(8):
                p = 8 * i + q
                product = across(stacked(state[level, p]), tiles[level, 0, p])
                held[p, :, :both] = product[:count] + product[count:]
            return carry

        lax.fori_loop(0, pairs // 8, step, 0)

    def combine(level, p):
        product = across(stacked(far[level, p]), tiles[level, 1, p])
        state[level + 1, p, :, :both] = held[p, :, :both] + (product[:count] + product[count:])

    def members(j):
        first, n = parts[j]
        return range(first, first + n)

    for j in range(len(parts)):
        src_copy(j).wait()
        leaf_copy(j).wait()
        if j + 2 < len(parts):
            load(j + 2)
        if j == 1:
            raw_copy(0).wait()
            raw_copy(1).wait()
        for p in members(j):
            compress(p)
        if j:
            for p in members(j - 1):
                lay(0, 0, p)
            for p in members(j - 1):
                pair_up(p)
            if j == 1:
                pl.semaphore_wait(barrier, levels - 1)
            exchange(1, j - 1).start()
    last = len(parts) - 1
    for p in members(last):
        lay(0, 0, p)
    for p in members(last):
        pair_up(p)
    exchange(1, last).start()
    for i in range(2, 2 * levels):
        raw_copy(i).start()
    for j in range(len(parts)):
        basis_copy(j).start()
    lay_level(1)
    own_term(1)
    lay_level(2)
    ahead = {1: (3,), 2: (4,), 3: (5, 6), 4: (), 5: (7,)}

    for level in range(1, levels):
        for j in range(len(parts)):
            exchange(level, j).wait_recv()
            for p in members(j):
                combine(level, p)
            if level + 1 < levels:
                exchange(level + 1, j).start()
            else:
                for p in members(j):

                    @pl.when(p != gy)
                    def _(p=p):
                        handover(p).start()

        if level + 1 < levels:
            own_term(level + 1)
        for later in ahead.get(level, ()):
            if later < levels:
                lay_level(later)
        if level == 1:
            for j in range(len(parts)):
                basis_copy(j).wait()

            def spread(p, carry):
                high, low = split(leaf_v[p])
                wide[p, :both] = high
                wide[p, both:] = low
                return carry

            lax.fori_loop(0, pairs, spread, 0)

    moved[gy] = state[levels, gy]

    def expand(a):
        high, low = split(moved[a][:, :both])
        none = jnp.zeros_like(high)
        rows = []
        for mine in (first_box, jnp.logical_not(first_box)):
            kept = jnp.where(mine, high, none)
            rows.append(jnp.concatenate([kept, kept], 1))
            rows.append(jnp.concatenate([jnp.where(mine, low, none), none], 1))
        product = jnp.dot(jnp.concatenate(rows, 0), wide[a], preferred_element_type=F32)
        for c in range(2):
            at = pl.multiple_of((2 * a + c) * points, points)
            out[:, pl.ds(at, points)] = (
                product[2 * c * count : (2 * c + 1) * count]
                + product[(2 * c + 1) * count : (2 * c + 2) * count]
            )

    hops = [0, 1, 2, 1]
    for far_off in range(5):
        ring = [d for d in range(n_gy) if hops[d % 4] + hops[d // 4 % 4] == far_off]
        sources = [crossed(gy, d) for d in ring]
        if far_off:
            for a in sources:
                arrival(a).wait_recv()
        for a in sources:
            expand(a)

    for level in range(1, levels):
        for j in range(len(parts)):
            exchange(level, j).wait_send()

    def drain(b, carry):
        @pl.when(b != gy)
        def _():
            handover(b).wait_send()

        return carry

    lax.fori_loop(0, n_gy, drain, 0)


def body(n_gx, n_gy, sources, leaf_basis, level_blocks, out_basis):
    boxes, rank, points = leaf_basis.shape
    count = sources.shape[0]
    levels = level_blocks.shape[0]
    pairs = boxes // 2
    parts = len(parts_of(pairs))
    leaf = leaf_basis.reshape(pairs, 2 * rank, points)
    basis = out_basis.reshape(pairs, 2 * rank, points)
    blocks = level_blocks.transpose(0, 1, 2, 4, 3).reshape(2 * levels, rank, boxes, rank)
    dma = pltpu.SemaphoreType.DMA
    anywhere = pl.BlockSpec(memory_space=pl.ANY)
    return pl.pallas_call(
        functools.partial(kernel, n_gx, n_gy, rank),
        out_shape=pltpu.VMEM((count, boxes * points), F32),
        in_specs=[anywhere] * 4,
        out_specs=pl.BlockSpec(memory_space=pltpu.VMEM),
        scratch_shapes=[
            pltpu.VMEM((count, boxes * points), F32),
            pltpu.VMEM((pairs, 2 * rank, points), F32),
            pltpu.VMEM((2 * levels, rank, boxes + 8, rank), F32),
            pltpu.VMEM((levels, 2, pairs, 2 * rank, 2 * LANES), BF16),
            pltpu.VMEM((levels + 1, pairs, count, LANES), F32),
            pltpu.VMEM((levels, pairs, count, LANES), F32),
            pltpu.VMEM((pairs, count, LANES), F32),
            pltpu.VMEM((n_gy, count, LANES), F32),
            pltpu.VMEM((pairs, 4 * rank, points), BF16),
            dma((parts,)),
            dma((parts,)),
            dma((2 * levels,)),
            dma((parts,)),
            dma((levels, parts)),
            dma((levels, parts)),
            dma((n_gy,)),
            dma((n_gy,)),
        ],
        compiler_params=pltpu.CompilerParams(
            collective_id=0, has_side_effects=True, vmem_limit_bytes=60 * 2**20
        ),
        name="sweep",
    )(sources, leaf, blocks, basis)


def solution(mesh):
    placed = (
        P(None, ("gx", "gy")),
        P(("gx", "gy"), None, None),
        P(None, None, None, None, ("gx", "gy")),
        P(("gx", "gy"), None, None),
    )
    return jax.shard_map(
        functools.partial(body, mesh.shape["gx"], mesh.shape["gy"]),
        mesh=mesh, in_specs=placed, out_specs=P(None, ("gx", "gy")), check_vma=False,
    )
```

```python
import functools

import jax
import jax.numpy as jnp
from jax import lax
from jax.experimental import pallas as pl
from jax.experimental.pallas import tpu as pltpu
from jax.sharding import PartitionSpec as P

F32 = jnp.float32
BF16 = jnp.bfloat16
LANES = 128
SHARES = (4, 3, 3, 3, 3)
LOADS = (1, 1, 2, 2, 2, 2, 2, 2, 2)
AHEAD = 4
DONE = 2


def parts_of(pairs, shares):
    if sum(shares) != pairs:
        return [(p, 1) for p in range(pairs)]
    return [(sum(shares[:j]), n) for j, n in enumerate(shares)]


def flipped(index, bit):
    return index + bit * (1 - 2 * (lax.div(index, bit) % 2))


def crossed(index, mask):
    bit = 1
    while bit <= mask:
        if mask & bit:
            index = flipped(index, bit)
        bit *= 2
    return index


def split(value):
    high = value.astype(BF16)
    return high, (value - high.astype(F32)).astype(BF16)


def stacked(value):
    high, low = split(value)
    return jnp.concatenate(
        [
            jnp.concatenate([high, high], 1),
            jnp.concatenate([low, jnp.zeros_like(low)], 1),
        ],
        0,
    )


def across(left, right):
    return lax.dot_general(left, right, (((1,), (1,)), ((), ())), preferred_element_type=F32)


HOPS = (0, 1, 2, 1)


def at_distance(gy, n_gy, low, high):
    away = [HOPS[d % 4] + HOPS[d // 4 % 4] for d in range(n_gy)]
    near = sorted((away[d], d) for d in range(n_gy) if low <= away[d] <= high)
    return [crossed(gy, d) for _, d in near]


def expanded(arrived, factors, rank):
    count = arrived.shape[0]
    both = 2 * rank
    first_box = lax.broadcasted_iota(jnp.int32, (count, both), 1) < rank
    high, low = split(arrived[:, :both])
    none = jnp.zeros_like(high)
    rows = []
    for mine in (first_box, jnp.logical_not(first_box)):
        kept = jnp.where(mine, high, none)
        rows.append(jnp.concatenate([kept, kept], 1))
        rows.append(jnp.concatenate([jnp.where(mine, low, none), none], 1))
    product = jnp.dot(jnp.concatenate(rows, 0), factors, preferred_element_type=F32)
    return [
        product[2 * c * count : (2 * c + 1) * count] + product[(2 * c + 1) * count : (2 * c + 2) * count]
        for c in range(2)
    ]


def finish(n_gy, rank, part, moved, wide, out, rest, part_sem, rest_sem):
    gy = lax.axis_index("gy")
    points = wide.shape[2]

    def place(a):
        return pl.ds(pl.multiple_of(a * 2 * points, 2 * points), 2 * points)

    copies = []
    for i, a in enumerate(at_distance(gy, n_gy, 0, DONE)):
        copies.append(pltpu.make_async_copy(part.at[:, place(a)], out.at[:, place(a)], part_sem.at[i]))
        copies[-1].start()
    for i, a in enumerate(at_distance(gy, n_gy, DONE + 1, 4)):
        boxes = expanded(moved[a], wide[a], rank)
        for c in range(2):
            rest[i, :, c * points : (c + 1) * points] = boxes[c]
        copies.append(pltpu.make_async_copy(rest.at[i], out.at[:, place(a)], rest_sem.at[i]))
        copies[-1].start()
    for copy in copies:
        copy.wait()


def kernel(
    n_gx, n_gy, rank,
    src, leaf, blocks, basis, out, moved, wide,
    src_v, leaf_v, raw, tiles, state, far, held,
    src_sem, leaf_sem, raw_sem, basis_sem, send_sem, recv_sem, out_sem, in_sem,
):
    pairs = leaf.shape[0]
    count = src.shape[0]
    points = leaf.shape[2]
    levels = blocks.shape[0] // 2
    parts = parts_of(pairs, SHARES)
    loads = parts_of(pairs, LOADS)
    both = 2 * rank
    pitch = raw.shape[2]
    gx, gy = lax.axis_index("gx"), lax.axis_index("gy")
    lane = lax.broadcasted_iota(jnp.int32, (count, both), 1)
    first_box = lane < rank

    def partner(level):
        bit = 2 ** (level - 1)
        if bit < n_gy:
            return gx, flipped(gy, bit)
        return flipped(gx, bit // n_gy), gy

    def src_copy(i):
        first, n = loads[i]
        here = pl.ds(first * 2 * points, n * 2 * points)
        return pltpu.make_async_copy(src.at[:, here], src_v.at[:, here], src_sem.at[i])

    def leaf_copy(i):
        here = pl.ds(*loads[i])
        return pltpu.make_async_copy(leaf.at[here], leaf_v.at[here], leaf_sem.at[i])

    def basis_copy(j):
        here = pl.ds(*parts[j])
        return pltpu.make_async_copy(basis.at[here], leaf_v.at[here], basis_sem.at[j])

    def raw_copy(i):
        return pltpu.make_async_copy(
            blocks.at[i], raw.at[i, :, pl.ds(0, 2 * pairs), :], raw_sem.at[i]
        )

    def exchange(level, j):
        here = pl.ds(*parts[j])
        return pltpu.make_async_remote_copy(
            src_ref=state.at[level, here],
            dst_ref=far.at[level, here],
            send_sem=send_sem.at[level, j],
            recv_sem=recv_sem.at[level, j],
            device_id=partner(level),
            device_id_type=pl.DeviceIdType.MESH,
        )

    def handover(b):
        return pltpu.make_async_remote_copy(
            src_ref=state.at[levels, b],
            dst_ref=moved.at[gy],
            send_sem=out_sem.at[b],
            recv_sem=in_sem.at[gy],
            device_id=(gx, b),
            device_id_type=pl.DeviceIdType.MESH,
        )

    def arrival(a):
        return pltpu.make_async_remote_copy(
            src_ref=state.at[levels, a],
            dst_ref=moved.at[a],
            send_sem=out_sem.at[a],
            recv_sem=in_sem.at[a],
            device_id=(gx, a),
            device_id_type=pl.DeviceIdType.MESH,
        )

    barrier = pltpu.get_barrier_semaphore()
    for level in range(1, levels):
        pl.semaphore_signal(barrier, inc=1, device_id=partner(level), device_id_type=pl.DeviceIdType.MESH)

    def load(i):
        src_copy(i).start()
        leaf_copy(i).start()

    def fetch(level):
        raw_copy(2 * level).start()
        raw_copy(2 * level + 1).start()

    for i in range(min(AHEAD, len(loads))):
        load(i)

    def blank(i, carry):
        state[i] = jnp.zeros_like(state[i])
        return carry

    lax.fori_loop(0, levels + 1, blank, 0)

    def lay(level, which, p):
        gap = jnp.zeros((rank, LANES - rank), F32)

        def rows_of(i, c):
            rows = raw.at[i].reshape(rank * pitch, rank)
            own = rows[pl.ds(2 * p + c, rank, stride=pitch), :]
            return jnp.concatenate([own, gap], 1)

        for c in range(2):
            full = rows_of(2 * level + which, c)
            if c:
                full = pltpu.roll(full, rank, 1)
            if level == 0:
                other = rows_of(1, c)
                full += other if c else pltpu.roll(other, rank, 1)
            high, low = split(full)
            tiles[level, which, p, c * rank : (c + 1) * rank, :LANES] = high
            tiles[level, which, p, c * rank : (c + 1) * rank, LANES:] = low

    def lay_level(level):
        def step(i, carry):
            for q in range(2):
                for which in range(1 if level == 0 else 2):
                    lay(level, which, 2 * i + q)
            return carry

        raw_copy(2 * level).wait()
        raw_copy(2 * level + 1).wait()
        if level + 2 < levels:
            fetch(level + 2)
        lax.fori_loop(0, pairs // 2, step, 0)

    def compress(p):
        high, low = split(leaf_v[p])
        h0, l0 = split(src_v[:, 2 * p * points : (2 * p + 1) * points])
        h1, l1 = split(src_v[:, (2 * p + 1) * points : (2 * p + 2) * points])
        main = across(jnp.concatenate([h0, h1, l0, l1], 0), high)
        rest = across(jnp.concatenate([h0, h1], 0), low)
        total = main[: 2 * count] + main[2 * count :] + rest
        state[0, p, :, :both] = jnp.where(first_box, total[:count], total[count:])

    def pair_up(p):
        product = across(stacked(state[0, p]), tiles[0, 0, p])
        state[1, p, :, :both] = product[:count] + product[count:]

    def own_term(level):
        def step(i, carry):
            for q in range(8):
                p = 8 * i + q
                product = across(stacked(state[level, p]), tiles[level, 0, p])
                held[p, :, :both] = product[:count] + product[count:]
            return carry

        lax.fori_loop(0, pairs // 8, step, 0)

    def combine(level, p):
        product = across(stacked(far[level, p]), tiles[level, 1, p])
        state[level + 1, p, :, :both] = held[p, :, :both] + (product[:count] + product[count:])

    def members(j):
        first, n = parts[j]
        return range(first, first + n)

    last = len(parts) - 1
    next_load = 0
    for j in range(len(parts)):
        if j == 1:
            raw_copy(0).wait()
            raw_copy(1).wait()
        while next_load < len(loads) and loads[next_load][0] < sum(parts[j]):
            src_copy(next_load).wait()
            leaf_copy(next_load).wait()
            if next_load == 0:
                fetch(0)
            if next_load + AHEAD < len(loads):
                load(next_load + AHEAD)
            elif next_load + AHEAD == len(loads):
                fetch(1)
            elif next_load + AHEAD == len(loads) + 1:
                fetch(2)
            if j == 0:
                for p in range(loads[next_load][0], sum(loads[next_load])):
                    compress(p)
            next_load += 1
        if j:
            for p in members(j):
                compress(p)
            for p in members(j - 1):
                lay(0, 0, p)
            if j == last:
                for p in members(last):
                    lay(0, 0, p)
            for p in members(j - 1):
                pair_up(p)
            if j == 1:
                pl.semaphore_wait(barrier, levels - 1)
            exchange(1, j - 1).start()
    for p in members(last):
        pair_up(p)
    exchange(1, last).start()
    lay_level(1)
    own_term(1)
    lay_level(2)
    for j in range(len(parts)):
        basis_copy(j).start()
    ahead = {1: (3,), 2: (4,), 3: (5, 6), 4: (), 5: (7,)}

    for level in range(1, levels):
        for j in range(len(parts)):
            exchange(level, j).wait_recv()
            for p in members(j):
                combine(level, p)
            if level + 1 < levels:
                exchange(level + 1, j).start()
            else:
                for p in members(j):

                    @pl.when(p != gy)
                    def _(p=p):
                        handover(p).start()

        if level + 1 < levels:
            own_term(level + 1)
        for later in ahead.get(level, ()):
            if later < levels:
                lay_level(later)
        if level == 3:
            for j in range(len(parts)):
                basis_copy(j).wait()

            def spread(p, carry):
                high, low = split(leaf_v[p])
                wide[p, :both] = high
                wide[p, both:] = low
                return carry

            lax.fori_loop(0, pairs, spread, 0)

    moved[gy] = state[levels, gy]

    for hops in range(5):
        ring = at_distance(gy, n_gy, hops, hops)
        if hops:
            for a in ring:
                arrival(a).wait_recv()
        if hops <= DONE:
            for a in ring:
                outputs = expanded(moved[a], wide[a], rank)
                for c in range(2):
                    at = pl.multiple_of((2 * a + c) * points, points)
                    out[:, pl.ds(at, points)] = outputs[c]

    for level in range(1, levels):
        for j in range(len(parts)):
            exchange(level, j).wait_send()

    def drain(b, carry):
        @pl.when(b != gy)
        def _():
            handover(b).wait_send()

        return carry

    lax.fori_loop(0, n_gy, drain, 0)


def body(n_gx, n_gy, sources, leaf_basis, level_blocks, out_basis):
    boxes, rank, points = leaf_basis.shape
    count = sources.shape[0]
    levels = level_blocks.shape[0]
    pairs = boxes // 2
    parts = len(parts_of(pairs, SHARES))
    loads = len(parts_of(pairs, LOADS))
    leaf = leaf_basis.reshape(pairs, 2 * rank, points)
    basis = out_basis.reshape(pairs, 2 * rank, points)
    blocks = level_blocks.transpose(0, 1, 2, 4, 3).reshape(2 * levels, rank, boxes, rank)
    dma = pltpu.SemaphoreType.DMA
    anywhere = pl.BlockSpec(memory_space=pl.ANY)
    held = pl.BlockSpec(memory_space=pltpu.VMEM)
    part, moved, wide = pl.pallas_call(
        functools.partial(kernel, n_gx, n_gy, rank),
        out_shape=(
            pltpu.VMEM((count, boxes * points), F32),
            pltpu.VMEM((n_gy, count, LANES), F32),
            pltpu.VMEM((pairs, 4 * rank, points), BF16),
        ),
        in_specs=[anywhere] * 4,
        out_specs=(held,) * 3,
        scratch_shapes=[
            pltpu.VMEM((count, boxes * points), F32),
            pltpu.VMEM((pairs, 2 * rank, points), F32),
            pltpu.VMEM((2 * levels, rank, boxes + 8, rank), F32),
            pltpu.VMEM((levels, 2, pairs, 2 * rank, 2 * LANES), BF16),
            pltpu.VMEM((levels + 1, pairs, count, LANES), F32),
            pltpu.VMEM((levels, pairs, count, LANES), F32),
            pltpu.VMEM((pairs, count, LANES), F32),
            dma((loads,)),
            dma((loads,)),
            dma((2 * levels,)),
            dma((parts,)),
            dma((levels, parts)),
            dma((levels, parts)),
            dma((n_gy,)),
            dma((n_gy,)),
        ],
        compiler_params=pltpu.CompilerParams(
            collective_id=0, has_side_effects=True, vmem_limit_bytes=46 * 2**20
        ),
        name="sweep",
    )(sources, leaf, blocks, basis)
    late = sum(HOPS[d % 4] + HOPS[d // 4 % 4] > DONE for d in range(n_gy))
    return pl.pallas_call(
        functools.partial(finish, n_gy, rank),
        out_shape=jax.ShapeDtypeStruct((count, boxes * points), F32),
        in_specs=[held] * 3,
        out_specs=anywhere,
        scratch_shapes=[
            pltpu.VMEM((max(late, 1), count, 2 * points), F32),
            dma((n_gy - late,)),
            dma((max(late, 1),)),
        ],
        compiler_params=pltpu.CompilerParams(vmem_limit_bytes=8 * 2**20),
        name="finish",
    )(part, moved, wide)


def solution(mesh):
    placed = (
        P(None, ("gx", "gy")),
        P(("gx", "gy"), None, None),
        P(None, None, None, None, ("gx", "gy")),
        P(("gx", "gy"), None, None),
    )
    return jax.shard_map(
        functools.partial(body, mesh.shape["gx"], mesh.shape["gy"]),
        mesh=mesh, in_specs=placed, out_specs=P(None, ("gx", "gy")), check_vma=False,
    )
```

```python
import functools

import jax
import jax.numpy as jnp
from jax import lax
from jax.experimental import pallas as pl
from jax.experimental.pallas import tpu as pltpu
from jax.sharding import PartitionSpec as P

F32 = jnp.float32
BF16 = jnp.bfloat16
LANES = 128
SHARES = (3, 4, 3, 3, 3)
LOADS = (1, 1, 2, 2, 2, 2, 2, 2, 2)
AHEAD = 4
DONE = 2
NEAR = 3


def parts_of(pairs, shares):
    if sum(shares) != pairs:
        return [(p, 1) for p in range(pairs)]
    return [(sum(shares[:j]), n) for j, n in enumerate(shares)]


def flipped(index, bit):
    return index + bit * (1 - 2 * (lax.div(index, bit) % 2))


def crossed(index, mask):
    bit = 1
    while bit <= mask:
        if mask & bit:
            index = flipped(index, bit)
        bit *= 2
    return index


def split(value):
    high = value.astype(BF16)
    return high, (value - high.astype(F32)).astype(BF16)


def stacked(value):
    high, low = split(value)
    return jnp.concatenate(
        [
            jnp.concatenate([high, high], 1),
            jnp.concatenate([low, jnp.zeros_like(low)], 1),
        ],
        0,
    )


def across(left, right):
    return lax.dot_general(left, right, (((1,), (1,)), ((), ())), preferred_element_type=F32)


HOPS = (0, 1, 2, 1)


def at_distance(gy, n_gy, low, high):
    away = [HOPS[d % 4] + HOPS[d // 4 % 4] for d in range(n_gy)]
    near = sorted((away[d], d) for d in range(n_gy) if low <= away[d] <= high)
    return [crossed(gy, d) for _, d in near]


def expanded(arrived, factors, rank):
    count = arrived.shape[0]
    both = 2 * rank
    first_box = lax.broadcasted_iota(jnp.int32, (count, both), 1) < rank
    high, low = split(arrived[:, :both])
    none = jnp.zeros_like(high)
    rows = []
    for mine in (first_box, jnp.logical_not(first_box)):
        kept = jnp.where(mine, high, none)
        rows.append(jnp.concatenate([kept, kept], 1))
        rows.append(jnp.concatenate([jnp.where(mine, low, none), none], 1))
    product = jnp.dot(jnp.concatenate(rows, 0), factors, preferred_element_type=F32)
    return [
        product[2 * c * count : (2 * c + 1) * count] + product[(2 * c + 1) * count : (2 * c + 2) * count]
        for c in range(2)
    ]


def finish(n_gy, rank, part, moved, wide, out, rest, part_sem, rest_sem):
    gy = lax.axis_index("gy")
    points = wide.shape[2]

    def place(a):
        return pl.ds(pl.multiple_of(a * 2 * points, 2 * points), 2 * points)

    copies = []
    for i, a in enumerate(at_distance(gy, n_gy, 0, DONE)):
        copies.append(pltpu.make_async_copy(part.at[:, place(a)], out.at[:, place(a)], part_sem.at[i]))
        copies[-1].start()
    for i, a in enumerate(at_distance(gy, n_gy, DONE + 1, 4)):
        boxes = expanded(moved[a], wide[a], rank)
        for c in range(2):
            rest[i, :, c * points : (c + 1) * points] = boxes[c]
        copies.append(pltpu.make_async_copy(rest.at[i], out.at[:, place(a)], rest_sem.at[i]))
        copies[-1].start()
    for copy in copies:
        copy.wait()


def kernel(
    n_gx, n_gy, rank,
    src, leaf, blocks, basis, out, moved, wide,
    src_v, leaf_v, raw, tiles, state, far, held,
    src_sem, leaf_sem, raw_sem, basis_sem, send_sem, recv_sem, out_sem, in_sem,
):
    pairs = leaf.shape[0]
    count = src.shape[0]
    points = leaf.shape[2]
    levels = blocks.shape[0] // 2
    parts = parts_of(pairs, SHARES)
    loads = parts_of(pairs, LOADS)
    both = 2 * rank
    pitch = raw.shape[2]
    gx, gy = lax.axis_index("gx"), lax.axis_index("gy")
    lane = lax.broadcasted_iota(jnp.int32, (count, both), 1)
    first_box = lane < rank

    def partner(level):
        bit = 2 ** (level - 1)
        if bit < n_gy:
            return gx, flipped(gy, bit)
        return flipped(gx, bit // n_gy), gy

    def src_copy(i):
        first, n = loads[i]
        here = pl.ds(first * 2 * points, n * 2 * points)
        return pltpu.make_async_copy(src.at[:, here], src_v.at[:, here], src_sem.at[i])

    def leaf_copy(i):
        here = pl.ds(*loads[i])
        return pltpu.make_async_copy(leaf.at[here], leaf_v.at[here], leaf_sem.at[i])

    def basis_copy(j):
        here = pl.ds(*parts[j])
        return pltpu.make_async_copy(basis.at[here], leaf_v.at[here], basis_sem.at[j])

    def raw_copy(i):
        return pltpu.make_async_copy(
            blocks.at[i], raw.at[i, :, pl.ds(0, 2 * pairs), :], raw_sem.at[i]
        )

    def exchange(level, j):
        here = pl.ds(*parts[j])
        return pltpu.make_async_remote_copy(
            src_ref=state.at[level, here],
            dst_ref=far.at[level, here],
            send_sem=send_sem.at[level, j],
            recv_sem=recv_sem.at[level, j],
            device_id=partner(level),
            device_id_type=pl.DeviceIdType.MESH,
        )

    def handover(b):
        return pltpu.make_async_remote_copy(
            src_ref=state.at[levels, b],
            dst_ref=moved.at[gy],
            send_sem=out_sem.at[b],
            recv_sem=in_sem.at[gy],
            device_id=(gx, b),
            device_id_type=pl.DeviceIdType.MESH,
        )

    def arrival(a):
        return pltpu.make_async_remote_copy(
            src_ref=state.at[levels, a],
            dst_ref=moved.at[a],
            send_sem=out_sem.at[a],
            recv_sem=in_sem.at[a],
            device_id=(gx, a),
            device_id_type=pl.DeviceIdType.MESH,
        )

    barrier = pltpu.get_barrier_semaphore()
    for level in range(1, levels):
        pl.semaphore_signal(barrier, inc=1, device_id=partner(level), device_id_type=pl.DeviceIdType.MESH)

    def load(i):
        src_copy(i).start()
        leaf_copy(i).start()

    def fetch(level):
        raw_copy(2 * level).start()
        raw_copy(2 * level + 1).start()

    for i in range(min(AHEAD, len(loads))):
        load(i)

    def blank(i, carry):
        state[i] = jnp.zeros_like(state[i])
        return carry

    lax.fori_loop(0, levels + 1, blank, 0)

    def lay(level, which, p):
        gap = jnp.zeros((rank, LANES - rank), F32)

        def rows_of(i, c):
            rows = raw.at[i].reshape(rank * pitch, rank)
            own = rows[pl.ds(2 * p + c, rank, stride=pitch), :]
            return jnp.concatenate([own, gap], 1)

        for c in range(2):
            full = rows_of(2 * level + which, c)
            if c:
                full = pltpu.roll(full, rank, 1)
            if level == 0:
                other = rows_of(1, c)
                full += other if c else pltpu.roll(other, rank, 1)
            high, low = split(full)
            tiles[level, which, p, c * rank : (c + 1) * rank, :LANES] = high
            tiles[level, which, p, c * rank : (c + 1) * rank, LANES:] = low

    def lay_level(level):
        def step(i, carry):
            for q in range(2):
                for which in range(1 if level == 0 else 2):
                    lay(level, which, 2 * i + q)
            return carry

        raw_copy(2 * level).wait()
        raw_copy(2 * level + 1).wait()
        if level + 2 < levels:
            fetch(level + 2)
        lax.fori_loop(0, pairs // 2, step, 0)

    def compress(p):
        high, low = split(leaf_v[p])
        h0, l0 = split(src_v[:, 2 * p * points : (2 * p + 1) * points])
        h1, l1 = split(src_v[:, (2 * p + 1) * points : (2 * p + 2) * points])
        main = across(jnp.concatenate([h0, h1, l0, l1], 0), high)
        rest = across(jnp.concatenate([h0, h1], 0), low)
        total = main[: 2 * count] + main[2 * count :] + rest
        state[0, p, :, :both] = jnp.where(first_box, total[:count], total[count:])

    def pair_up(p):
        product = across(stacked(state[0, p]), tiles[0, 0, p])
        state[1, p, :, :both] = product[:count] + product[count:]

    def own_term(level):
        def step(i, carry):
            for q in range(8):
                p = 8 * i + q
                product = across(stacked(state[level, p]), tiles[level, 0, p])
                held[p, :, :both] = product[:count] + product[count:]
            return carry

        lax.fori_loop(0, pairs // 8, step, 0)

    def combine(level, p):
        product = across(stacked(far[level, p]), tiles[level, 1, p])
        state[level + 1, p, :, :both] = held[p, :, :both] + (product[:count] + product[count:])

    def combine_both(level, p):
        product = across(stacked(state[level, p]), tiles[level, 0, p])
        product += across(stacked(far[level, p]), tiles[level, 1, p])
        state[level + 1, p, :, :both] = product[:count] + product[count:]

    def members(j):
        first, n = parts[j]
        return range(first, first + n)

    last = len(parts) - 1
    next_load = 0
    for j in range(len(parts)):
        if j == 1:
            raw_copy(0).wait()
            raw_copy(1).wait()
        while next_load < len(loads) and loads[next_load][0] < sum(parts[j]):
            src_copy(next_load).wait()
            leaf_copy(next_load).wait()
            if next_load == 0:
                fetch(0)
            if next_load + AHEAD < len(loads):
                load(next_load + AHEAD)
            elif next_load + AHEAD == len(loads):
                fetch(1)
            elif next_load + AHEAD == len(loads) + 1:
                fetch(2)
            if j == 0:
                for p in range(loads[next_load][0], sum(loads[next_load])):
                    compress(p)
            next_load += 1
        if j:
            for p in members(j):
                compress(p)
            for p in members(j - 1):
                lay(0, 0, p)
            if j == last:
                for p in members(last):
                    lay(0, 0, p)
            for p in members(j - 1):
                pair_up(p)
            if j == 1:
                pl.semaphore_wait(barrier, levels - 1)
            exchange(1, j - 1).start()
    for p in members(last):
        pair_up(p)
    exchange(1, last).start()
    lay_level(1)
    own_term(1)
    for j in range(len(parts)):
        basis_copy(j).start()
    ahead = {1: (3,), 2: (4,), 3: (5, 6), 4: (), 5: (7,)}

    near = 1 + (n_gy.bit_length() - 1)
    for level in range(1, levels):
        groups = [[j] for j in range(len(parts))]
        if level == near:
            groups = [range(NEAR), range(NEAR, len(parts))]
        for group in groups:
            for j in group:
                exchange(level, j).wait_recv()
            for j in group:
                for p in members(j):
                    if level == near:
                        combine_both(level, p)
                    else:
                        combine(level, p)
            for j in group:
                if level + 1 < levels:
                    exchange(level + 1, j).start()
                else:
                    for p in members(j):

                        @pl.when(p != gy)
                        def _(p=p):
                            handover(p).start()

        if level == 1:
            lay_level(2)
        if level + 1 < levels and level + 1 != near:
            own_term(level + 1)
        for later in ahead.get(level, ()):
            if later < levels:
                lay_level(later)
        if level == levels - 2:
            for j in range(len(parts)):
                basis_copy(j).wait()

            def spread(p, carry):
                high, low = split(leaf_v[p])
                wide[p, :both] = high
                wide[p, both:] = low
                return carry

            lax.fori_loop(0, pairs, spread, 0)

    moved[gy] = state[levels, gy]

    for hops in range(5):
        ring = at_distance(gy, n_gy, hops, hops)
        if hops:
            for a in ring:
                arrival(a).wait_recv()
        if hops <= DONE:
            for a in ring:
                outputs = expanded(moved[a], wide[a], rank)
                for c in range(2):
                    at = pl.multiple_of((2 * a + c) * points, points)
                    out[:, pl.ds(at, points)] = outputs[c]

    for level in range(1, levels):
        for j in range(len(parts)):
            exchange(level, j).wait_send()

    def drain(b, carry):
        @pl.when(b != gy)
        def _():
            handover(b).wait_send()

        return carry

    lax.fori_loop(0, n_gy, drain, 0)


def body(n_gx, n_gy, sources, leaf_basis, level_blocks, out_basis):
    boxes, rank, points = leaf_basis.shape
    count = sources.shape[0]
    levels = level_blocks.shape[0]
    pairs = boxes // 2
    parts = len(parts_of(pairs, SHARES))
    loads = len(parts_of(pairs, LOADS))
    leaf = leaf_basis.reshape(pairs, 2 * rank, points)
    basis = out_basis.reshape(pairs, 2 * rank, points)
    blocks = level_blocks.transpose(0, 1, 2, 4, 3).reshape(2 * levels, rank, boxes, rank)
    dma = pltpu.SemaphoreType.DMA
    anywhere = pl.BlockSpec(memory_space=pl.ANY)
    held = pl.BlockSpec(memory_space=pltpu.VMEM)
    part, moved, wide = pl.pallas_call(
        functools.partial(kernel, n_gx, n_gy, rank),
        out_shape=(
            pltpu.VMEM((count, boxes * points), F32),
            pltpu.VMEM((n_gy, count, LANES), F32),
            pltpu.VMEM((pairs, 4 * rank, points), BF16),
        ),
        in_specs=[anywhere] * 4,
        out_specs=(held,) * 3,
        scratch_shapes=[
            pltpu.VMEM((count, boxes * points), F32),
            pltpu.VMEM((pairs, 2 * rank, points), F32),
            pltpu.VMEM((2 * levels, rank, boxes + 8, rank), F32),
            pltpu.VMEM((levels, 2, pairs, 2 * rank, 2 * LANES), BF16),
            pltpu.VMEM((levels + 1, pairs, count, LANES), F32),
            pltpu.VMEM((levels, pairs, count, LANES), F32),
            pltpu.VMEM((pairs, count, LANES), F32),
            dma((loads,)),
            dma((loads,)),
            dma((2 * levels,)),
            dma((parts,)),
            dma((levels, parts)),
            dma((levels, parts)),
            dma((n_gy,)),
            dma((n_gy,)),
        ],
        compiler_params=pltpu.CompilerParams(
            collective_id=0, has_side_effects=True, vmem_limit_bytes=46 * 2**20
        ),
        name="sweep",
    )(sources, leaf, blocks, basis)
    late = sum(HOPS[d % 4] + HOPS[d // 4 % 4] > DONE for d in range(n_gy))
    return pl.pallas_call(
        functools.partial(finish, n_gy, rank),
        out_shape=jax.ShapeDtypeStruct((count, boxes * points), F32),
        in_specs=[held] * 3,
        out_specs=anywhere,
        scratch_shapes=[
            pltpu.VMEM((max(late, 1), count, 2 * points), F32),
            dma((n_gy - late,)),
            dma((max(late, 1),)),
        ],
        compiler_params=pltpu.CompilerParams(vmem_limit_bytes=8 * 2**20),
        name="finish",
    )(part, moved, wide)


def solution(mesh):
    placed = (
        P(None, ("gx", "gy")),
        P(("gx", "gy"), None, None),
        P(None, None, None, None, ("gx", "gy")),
        P(("gx", "gy"), None, None),
    )
    return jax.shard_map(
        functools.partial(body, mesh.shape["gx"], mesh.shape["gy"]),
        mesh=mesh, in_specs=placed, out_specs=P(None, ("gx", "gy")), check_vma=False,
    )
```
